256 devices in a mesh: dp: 16 (over z, y_lo), mp: 16 (over x, y_hi, core).
Axes of the slice: x: 4, y: 4 (y_hi: 2, y_lo: 2; y = y_hi * 2 + y_lo), z: 8, core: 2. Of those that a mesh axis runs over, the one named last changes fastest.
Arguments:
- pre_act: bfloat16 [2048, 36864], P('dp', 'mp'), may hold values from -6 to 6
- grad_out: bfloat16 [2048, 18432], P('dp', 'mp'), may hold values from -6 to 6
- row_state: float32 [16, 1152], P(None, 'dp'), may hold values from 3e-05 to 0.0003
- col_state: float32 [36864], P('mp'), may hold values from 3e-05 to 0.0003
Outputs:
- update: bfloat16 [16, 1152, 36864], P(None, 'dp', 'mp')
- row_new: float32 [16, 1152], P(None, 'dp')
- col_new: float32 [36864], P('mp')
The draws below stay inside these ranges and needn't reach their ends.
All inputs are finite; a program needn't handle non-finite values.
Results may differ from the reference program's by a relative error of at most 0.0015.
The reference program's roundings to bfloat16 on the way (of `hidden`) count: a program that leaves them out, or rounds other values in their place, can miss the bound.
Values may be sent and summed in bfloat16 or wider, within the bound.
No kernel may reach another device: no remote copies, remote signals or barrier semaphores. Data moves between devices by JAX's collectives and lax.ppermute only.
A program may use at most 128 MiB of HBM per device.

```python
import math
import jax
import jax.numpy as jnp
from jax import lax

D = 18432
FFW = 36864
TOKENS = 2048
N_MP = 16


def raised(array, rng, source, target, shards_of, factor):
    def block_of(position):
        return (jnp.arange(array.shape[position]) // (array.shape[position] // shards_of)).reshape((-1,) + (1,) * (array.ndim - 1 - position))

    near = jax.random.permutation(rng, shards_of)[block_of(target)]
    other_side = (block_of(target) + shards_of // 2) % shards_of
    return jnp.where((block_of(source) == near) | (block_of(source) == other_side), factor * array, array)


def level_of(key, dims, shards, smallest, top_value):
    def one(dim, shards_of):
        steps = jax.random.uniform(jax.random.fold_in(jax.random.fold_in(key, 6), dim), (shards_of,), jnp.float32, smallest / len(shards), top_value / len(shards))
        return jnp.repeat(jnp.exp(steps), dims[dim] // shards_of).reshape((-1,) + (1,) * (len(dims) - dim - 1))

    factor_of = one(*shards[0])
    for cut in shards[1:]:
        factor_of = factor_of * one(*cut)
    return factor_of


def normal_values(rng, extent, spread, reach, split=(), dtype=jnp.bfloat16):
    level = level_of(rng, extent, split, -0.22, 0.18) if split else 1.0
    entries = jax.random.normal(rng, extent, jnp.float32) * spread * level
    return jnp.minimum(jnp.maximum(entries, -reach), reach).astype(dtype)


def gaussian_with(key, shape, scale, bound, cuts, heavy, kind=jnp.bfloat16):
    result = scale * jax.random.normal(key, shape, jnp.float32)
    if cuts:
        result = result * level_of(key, shape, cuts, -0.22, 0.18)
    return jnp.clip(raised(result, jax.random.fold_in(key, 3), *heavy), -bound, bound).astype(kind)


def setup_inputs(seed: int = 0) -> dict:
    key_of = jax.random.split(jax.random.key(seed), 5)
    pre_act = normal_values(key_of[0], (TOKENS, FFW), 1.0, 6.0, ((0, 16), (1, 16)))
    grad_out = gaussian_with(key_of[1], (TOKENS, D), 1.0, 6.0, ((0, 16), (1, 16)), (0, 1, 16, 2.0))
    row_state = jnp.clip(jnp.exp(math.log(0.0003) - 2.3025852 * jax.random.uniform(key_of[2], (N_MP, D // N_MP), jnp.float32) ** level_of(key_of[2], (N_MP, D // N_MP), ((1, 16),), -0.2, 0.2)), 2.9999999242136255e-05, 0.0003)
    col_state = jnp.clip(jnp.exp(math.log(0.0003) - 2.3025852 * jax.random.uniform(key_of[3], (FFW,), jnp.float32) ** level_of(key_of[3], (FFW,), ((0, 16),), -0.2, 0.2)), 2.9999999242136255e-05, 0.0003)
    return dict(pre_act=pre_act, grad_out=grad_out, row_state=row_state, col_state=col_state)


decay = 1.0 - 2.0 ** (-0.8)
tiny = 1e-30

def reference(pre_act, grad_out, row_state, col_state):
    hidden = jax.nn.gelu(pre_act.astype(jnp.float32)).astype(jnp.bfloat16)
    grad = jnp.dot(grad_out.T, hidden, preferred_element_type=jnp.float32) / TOKENS
    row_sum = lax.optimization_barrier(jnp.sum(grad * grad, axis=1))
    col_sum = lax.optimization_barrier(jnp.sum(grad * grad, axis=0))
    row_flat = row_state.reshape(D)
    row_new = decay * row_flat + (1.0 - decay) * (row_sum / FFW + tiny)
    col_new = decay * col_state + (1.0 - decay) * (col_sum / D + tiny)
    scale = jnp.mean(row_new)
    update = (grad * lax.rsqrt(row_new[:, None] * col_new[None, :] / scale)).astype(jnp.bfloat16)
    return (update.reshape(N_MP, D // N_MP, FFW), row_new.reshape(N_MP, D // N_MP), col_new)
```

```python
import jax
import jax.numpy as jnp
from jax import lax
from jax.sharding import Mesh, PartitionSpec as P

D = 18432

decay = 1.0 - 2.0 ** (-0.8)
tiny = 1e-30

DP = ("z", "yl")
DPR = ("yl", "z")
MP = ("x", "yh", "core")


def ring(n, s):
    return [(i, (i + s) % n) for i in range(n)]


def gather_mp(q):
    x = lax.axis_index("x")
    yh = lax.axis_index("yh")
    core = lax.axis_index("core")
    n = q.shape[0]
    other = lax.ppermute(q, "yh", ring(2, 1))
    pair = jnp.concatenate([q, other], 0)
    fwd = lax.ppermute(pair, "x", ring(4, 1))
    bwd = lax.ppermute(pair, "x", ring(4, -1))
    far_a = lax.ppermute(fwd[:n], "x", ring(4, 1))
    far_b = lax.ppermute(bwd[n:], "x", ring(4, -1))
    rel = jnp.stack([pair, fwd, jnp.concatenate([far_a, far_b], 0), bwd], 0)
    rel = rel.reshape((4, 2) + q.shape)
    theirs = lax.ppermute(rel, "core", ring(2, 1))
    both = jnp.stack([rel, theirs], 2)
    out = jnp.zeros((4, 2, 2) + q.shape, q.dtype)
    for rx in range(4):
        for ry in range(2):
            for rc in range(2):
                out = lax.dynamic_update_slice(
                    out,
                    both[rx, ry, rc][None, None, None],
                    ((x + 4 - rx) % 4, (yh + ry) % 2, (core + rc) % 2, 0, 0, 0),
                )
    return out.reshape((16,) + q.shape)


def spread_sum(v, axes, n):
    got = lax.all_to_all(jnp.broadcast_to(v[None], (n,) + v.shape), axes, 0, 0, tiled=True)
    return jnp.sum(got, axis=0)


def body(pre_act, grad_out, row_state, col_state):
    tok_rows, hid_cols = pre_act.shape
    all_tokens = tok_rows * 16
    all_hidden = hid_cols * 16
    width = row_state.shape[1]
    own = 16 * width
    hidden = jax.nn.gelu(pre_act.astype(jnp.float32)).astype(jnp.bfloat16)
    parts = 2
    pw = hid_cols // parts
    hid = [
        lax.all_gather(hidden[:, i * pw : (i + 1) * pw], DPR, axis=0, tiled=True)
        for i in range(parts)
    ]
    go = grad_out.T.reshape(8, 2, width, tok_rows).transpose(1, 0, 2, 3)
    go = go.reshape(16, width, tok_rows)
    q = lax.all_to_all(go, DPR, 0, 0, tiled=True)
    allq = gather_mp(q)
    lhs = allq.transpose(0, 2, 1, 3).reshape(own, all_tokens)
    grads = []
    rows = 0.0
    cols = []
    for h in hid:
        g = lax.dot_general(
            lhs, h, (((1,), (0,)), ((), ())), preferred_element_type=jnp.float32
        ) / all_tokens
        s = g * g
        rows = rows + jnp.sum(s, axis=1)
        cols.append(jnp.sum(s, axis=0))
        grads.append(g)
    row_sum = spread_sum(rows.reshape(16, width), MP, 16)
    row_new = decay * row_state + (1.0 - decay) * (row_sum / all_hidden + tiny)
    vec = jnp.concatenate(cols + [jnp.full((256,), jnp.sum(row_new), jnp.float32)])
    got = spread_sum(vec.reshape(20, 128), DP, 16).reshape(-1)
    col_new = decay * col_state + (1.0 - decay) * (got[:hid_cols] / D + tiny)
    scale = got[hid_cols] / D
    ups = []
    for i, g in enumerate(grads):
        c = col_new[i * pw : (i + 1) * pw]
        ups.append(
            (g * lax.rsqrt(row_new.reshape(own)[:, None] * c[None, :] / scale)).astype(
                jnp.bfloat16
            )
        )
    update = jnp.concatenate(ups, 1)
    return update.reshape(16, width, hid_cols), row_new, col_new


def solution(mesh):
    fine = Mesh(mesh.devices.reshape(8, 2, 4, 2, 2), ("z", "yl", "x", "yh", "core"))
    return jax.shard_map(
        body,
        mesh=fine,
        in_specs=(P(DP, MP), P(DP, MP), P(None, DP), P(MP)),
        out_specs=(P(None, DP, MP), P(None, DP), P(MP)),
        check_vma=False,
    )
```

```python
import functools

import jax
import jax.numpy as jnp
from jax import lax
from jax.experimental import pallas as pl
from jax.experimental.pallas import tpu as pltpu
from jax.sharding import Mesh, PartitionSpec as P

D = 18432

decay = 1.0 - 2.0 ** (-0.8)
tiny = 1e-30

DP = ("z", "yl")
MP = ("x", "yh", "core")

TOK = 128
HID = 2304
WID = 72
OWN = 1152
ALL_TOK = 2048
FFW = 36864
CB = 256
A_COLS = 1536
A_BLOCKS = A_COLS // CB
BLOCKS = HID // CB
A_HALF = A_COLS // 2
SPLIT = 1024
MIB = 1024 * 1024

ANY = pl.BlockSpec(memory_space=pl.ANY)
VMEM = pl.BlockSpec(memory_space=pltpu.VMEM)
SMEM = pl.BlockSpec(memory_space=pltpu.SMEM)


def ring(n, s):
    return [(i, (i + s) % n) for i in range(n)]


def send(v, axis, n, s):
    return lax.ppermute(v, axis, ring(n, s))


def lhs_kernel(pos, xp, f, b, fa, fb, cxp, cf, cb, cfa, cfb, out):
    x, yh, core = pos[2], pos[3], pos[4]
    for half, group in ((core, (xp, f, b, fa, fb)), (1 - core, (cxp, cf, cb, cfa, cfb))):
        gxp, gf, gb, gfa, gfb = group
        for ref, lead, dx, dy in (
            (gxp, 0, 0, 0),
            (gxp, 1, 0, 1),
            (gf, 0, 3, 0),
            (gf, 1, 3, 1),
            (gb, 0, 1, 0),
            (gb, 1, 1, 1),
            (gfa, None, 2, 0),
            (gfb, None, 2, 1),
        ):
            row = (lax.rem(x + dx, 4) * 2 + lax.rem(yh + dy, 2)) * (2 * WID)
            row = pl.multiple_of(row, 16)
            for i in range(8):
                block = ref[i] if lead is None else ref[lead, i]
                col = pl.multiple_of((half * 8 + i) * TOK, TOK)
                out[pl.ds(row, 2 * WID), pl.ds(col, TOK)] = block


def place_features(pos, mine, theirs):
    return pl.pallas_call(
        lhs_kernel,
        out_shape=jax.ShapeDtypeStruct((OWN, ALL_TOK), jnp.bfloat16),
        in_specs=[SMEM] + [VMEM] * 10,
        out_specs=VMEM,
        compiler_params=pltpu.CompilerParams(vmem_limit_bytes=50 * MIB),
        cost_estimate=pl.CostEstimate(
            flops=0, bytes_accessed=2 * OWN * ALL_TOK * 2, transcendentals=0
        ),
        name="features",
    )(pos, *mine, *theirs)


def tie(*v):
    return lax.optimization_barrier(v)


def up_z(v):
    return send(v, "z", 8, 1)


def down_z(v):
    return send(v, "z", 8, -1)


def other(v, axis):
    return send(v, axis, 2, 1)


def exchange(hidden, grad_out, pos):
    core = pos[4]

    def cross(*parts):
        return other(jnp.concatenate(parts, 0), "yl")

    def cut(v, first, last):
        return lax.slice_in_dim(v, first, last, axis=1)

    hidden, grad_out = tie(hidden, grad_out)
    u1, d1, near = up_z(hidden), down_z(hidden), other(hidden, "yl")
    turned = grad_out.T.reshape(16, WID, TOK)
    q = lax.all_to_all(turned, DP, 0, 0, tiled=True)
    u1, d1, near = tie(u1, d1, near)
    side = cut(near, 0, A_COLS)
    u2 = up_z(jnp.concatenate([u1, side], 1))
    d2 = down_z(jnp.concatenate([d1, side], 1))
    y1 = cross(cut(u1, A_COLS, HID), cut(d1, A_COLS, HID))
    keep = lax.dynamic_slice_in_dim(q, 8 * core, 8, 0)
    give = lax.dynamic_slice_in_dim(q, 8 - 8 * core, 8, 0)
    got = other(give, "core")
    first = jnp.where(core == 0, keep, got)
    second = jnp.where(core == 0, got, keep)
    half = jnp.concatenate([first, second], 1)
    far = other(half, "yh")
    u2, d2, y1, far = tie(u2, d2, y1, far)
    u3, d3 = up_z(u2), down_z(d2)
    xp = jnp.stack([half, far], 0)
    f, b = send(xp, "x", 4, 1), send(xp, "x", 4, -1)
    y2 = cross(cut(u2, A_COLS, HID), cut(d2, A_COLS, HID))
    cxp = other(xp, "core")
    u3, d3, y2, f, b, cxp = tie(u3, d3, y2, f, b, cxp)
    u4 = up_z(jnp.concatenate([cut(u3, 0, SPLIT), cut(u3, HID, HID + A_COLS)], 1))
    d4 = down_z(cut(d3, SPLIT, HID + A_COLS))
    fa, fb = send(f[0], "x", 4, 1), send(b[1], "x", 4, -1)
    cf, cb = other(f, "core"), other(b, "core")
    y3 = cross(cut(u3, A_COLS, HID), cut(d3, A_COLS, HID))
    u4, d4, y3, fa, fb, cf, cb = tie(u4, d4, y3, fa, fb, cf, cb)
    u5 = up_z(cut(u4, SPLIT, SPLIT + A_HALF))
    d5 = down_z(cut(d4, HID - SPLIT + A_HALF, HID - SPLIT + A_COLS))
    y4 = cross(cut(d4, A_COLS - SPLIT, HID - SPLIT))
    lhs = place_features(
        pos, (xp, f, b, fa, fb), (cxp, cf, cb, other(fa, "core"), other(fb, "core"))
    )
    n, m, h, k = BLOCKS, A_BLOCKS, SPLIT // CB, A_HALF // CB
    pieces = [
        (hidden, 0, 0, 0, 0, 0, n),
        (near, 0, 0, 0, 1, 0, n),
        (u1, 0, 0, 7, 0, 0, n),
        (d1, 0, 0, 1, 0, 0, n),
        (y1, 0, -A_COLS, 7, 1, m, n),
        (y1, TOK, -A_COLS, 1, 1, m, n),
        (u2, 0, 0, 6, 0, 0, n),
        (d2, 0, 0, 2, 0, 0, n),
        (u2, 0, HID, 7, 1, 0, m),
        (d2, 0, HID, 1, 1, 0, m),
        (y2, 0, -A_COLS, 6, 1, m, n),
        (y2, TOK, -A_COLS, 2, 1, m, n),
        (u3, 0, 0, 5, 0, 0, n),
        (d3, 0, 0, 3, 0, 0, n),
        (u3, 0, HID, 6, 1, 0, m),
        (d3, 0, HID, 2, 1, 0, m),
        (y3, 0, -A_COLS, 5, 1, m, n),
        (y3, TOK, -A_COLS, 3, 1, m, n),
        (u4, 0, 0, 4, 0, 0, h),
        (d4, 0, -SPLIT, 4, 0, h, n),
        (u4, 0, SPLIT, 5, 1, 0, m),
        (d4, 0, HID - SPLIT, 3, 1, 0, m),
        (y4, 0, -A_COLS, 4, 1, m, n),
        (u5, 0, 0, 4, 1, 0, k),
        (d5, 0, -A_HALF, 4, 1, k, m),
    ]
    return pieces, lhs


def product_kernel(plan, count, pos, lhs_hbm, *refs):
    arrays = refs[:count]
    grad, rows_out, cols_out = refs[count : count + 3]
    lhs, hid, outbuf, rowacc, lsem, hsem, osem = refs[count + 3 :]
    z, yl = pos[0], pos[1]

    def issue(j, slot):
        edges = sorted({p[5] for p in plan} | {p[6] for p in plan})
        for lo, hi in zip(edges[:-1], edges[1:]):

            @pl.when((j >= lo) & (j < hi))
            def _(lo=lo):
                for index, row, base, dz, dy, first, last in plan:
                    if not first <= lo < last:
                        continue
                    s = lax.rem(z + dz, 8) * 2 + lax.rem(yl + dy, 2)
                    col = pl.multiple_of(j * CB + base, CB)
                    pltpu.make_async_copy(
                        arrays[index].at[pl.ds(row, TOK), pl.ds(col, CB)],
                        hid.at[slot, pl.ds(pl.multiple_of(s * TOK, TOK), TOK), :],
                        hsem.at[slot],
                    ).start()

    pltpu.make_async_copy(lhs_hbm, lhs, lsem).start()
    issue(jnp.int32(0), 0)
    rowacc[...] = jnp.zeros_like(rowacc)
    pltpu.make_async_copy(lhs_hbm, lhs, lsem).wait()

    def out_copy(j, slot):
        return pltpu.make_async_copy(
            outbuf.at[slot],
            grad.at[:, pl.ds(pl.multiple_of(j * CB, CB), CB)],
            osem.at[slot],
        )

    def step(j, carry):
        slot = lax.rem(j, 2)

        @pl.when(j + 1 < BLOCKS)
        def _():
            issue(j + 1, 1 - slot)

        pltpu.make_async_copy(hid.at[slot], hid.at[slot], hsem.at[slot]).wait()

        @pl.when(j >= 2)
        def _():
            out_copy(j - 2, slot).wait()

        col = jnp.zeros((8, CB), jnp.float32)
        for r in range(0, OWN, 384):
            g = jnp.dot(
                lhs[r : r + 384, :], hid[slot], preferred_element_type=jnp.float32
            ) * (1.0 / ALL_TOK)
            outbuf[slot, r : r + 384, :] = g
            sq = g * g
            rowacc[r : r + 384, :] += sq[:, :128] + sq[:, 128:]
            col = col + jnp.sum(sq.reshape(48, 8, CB), axis=0)
        total = jnp.sum(col, axis=0, keepdims=True)
        cols_out[pl.ds(2 * j, 1), :] = total[:, :128]
        cols_out[pl.ds(2 * j + 1, 1), :] = total[:, 128:]
        out_copy(j, slot).start()
        return carry

    lax.fori_loop(0, BLOCKS, step, 0)
    for i in range(9):
        part = rowacc[i * 128 : (i + 1) * 128, :]
        line = jnp.sum(part.T, axis=0, keepdims=True)
        for d in range(16):
            rows_out[d, i : i + 1, :] = line
    out_copy(BLOCKS - 2, (BLOCKS - 2) % 2).wait()
    out_copy(BLOCKS - 1, (BLOCKS - 1) % 2).wait()


def product(lhs, pieces, pos):
    arrays = []
    plan = []
    for piece in pieces:
        index = [i for i, a in enumerate(arrays) if a is piece[0]]
        if not index:
            arrays.append(piece[0])
            index = [len(arrays) - 1]
        plan.append((index[0],) + piece[1:])
    return pl.pallas_call(
        functools.partial(product_kernel, plan, len(arrays)),
        out_shape=(
            jax.ShapeDtypeStruct((OWN, HID), jnp.float32),
            jax.ShapeDtypeStruct((16, 9, 128), jnp.float32),
            jax.ShapeDtypeStruct((18, 128), jnp.float32),
        ),
        in_specs=[SMEM] + [ANY] * (1 + len(arrays)),
        out_specs=(ANY, VMEM, VMEM),
        scratch_shapes=[
            pltpu.VMEM((OWN, ALL_TOK), jnp.bfloat16),
            pltpu.VMEM((2, ALL_TOK, CB), jnp.bfloat16),
            pltpu.VMEM((2, OWN, CB), jnp.float32),
            pltpu.VMEM((OWN, 128), jnp.float32),
            pltpu.SemaphoreType.DMA,
            pltpu.SemaphoreType.DMA((2,)),
            pltpu.SemaphoreType.DMA((2,)),
        ],
        compiler_params=pltpu.CompilerParams(vmem_limit_bytes=50 * MIB),
        cost_estimate=pl.CostEstimate(
            flops=2 * OWN * HID * ALL_TOK,
            bytes_accessed=OWN * HID * 4 + ALL_TOK * HID * 2,
            transcendentals=0,
        ),
        name="product",
    )(pos, lhs, *arrays)


def middle_kernel(got, row_state, cols, row_new, payload):
    row_sum = jnp.sum(got[...], axis=0)
    new = decay * row_state[...] + (1.0 - decay) * (row_sum / FFW + tiny)
    row_new[...] = new
    total = jnp.sum(jnp.sum(new, axis=0, keepdims=True), axis=1, keepdims=True)
    for d in range(16):
        payload[d, :18, :] = cols[...]
        payload[d, 18:, :] = jnp.broadcast_to(total, (6, 128))


STRIPES = 9


def update_kernel(got, row_new, col_state, grad, out, col_new, colf, gbuf, obuf, rsem, wsem):
    def read(i):
        rows = pl.ds(i * 128, 128)
        return pltpu.make_async_copy(grad.at[rows, :], gbuf.at[rows, :], rsem.at[i])

    def write(i):
        rows = pl.ds(i * 128, 128)
        return pltpu.make_async_copy(obuf.at[rows, :], out.at[rows, :], wsem.at[i])

    for i in range(STRIPES):
        read(i).start()
    sums = jnp.sum(got[...], axis=0)
    new = decay * col_state[...] + (1.0 - decay) * (sums[:18, :] / D + tiny)
    col_new[...] = new
    inv = lax.rsqrt(new)
    for k in range(18):
        colf[:, k * 128 : (k + 1) * 128] = jnp.broadcast_to(inv[k : k + 1, :], (8, 128))
    scale = sums[18:19, :] / D
    rowf = lax.rsqrt(row_new[...]) * jnp.sqrt(scale)
    for i in range(STRIPES):
        column = jnp.broadcast_to(rowf[i : i + 1, :], (128, 128)).T
        read(i).wait()
        for k in range(18):
            sl = slice(k * 128, (k + 1) * 128)
            obuf[i * 128 : (i + 1) * 128, sl] = (
                gbuf[i * 128 : (i + 1) * 128, sl] * (column * colf[0:1, sl])
            ).astype(jnp.bfloat16)
        write(i).start()
    for i in range(STRIPES):
        write(i).wait()


def spread(v, axes):
    return lax.all_to_all(v, axes, 0, 0, tiled=True)


def body(pre_act, grad_out, row_state, col_state):
    pos = jnp.stack([lax.axis_index(a) for a in ("z", "yl", "x", "yh", "core")]).astype(
        jnp.int32
    )
    hidden = jax.nn.gelu(pre_act.astype(jnp.float32)).astype(jnp.bfloat16)
    pieces, lhs = exchange(hidden, grad_out, pos)
    grad, rows, cols = product(lhs, pieces, pos)
    row_new, payload = pl.pallas_call(
        middle_kernel,
        out_shape=(
            jax.ShapeDtypeStruct((9, 128), jnp.float32),
            jax.ShapeDtypeStruct((16, 24, 128), jnp.float32),
        ),
        in_specs=[VMEM] * 3,
        out_specs=(VMEM, VMEM),
        compiler_params=pltpu.CompilerParams(vmem_limit_bytes=4 * MIB),
        name="middle",
    )(spread(rows, MP), row_state.reshape(9, 128), cols)
    update, col_new = pl.pallas_call(
        update_kernel,
        out_shape=(
            jax.ShapeDtypeStruct((OWN, HID), jnp.bfloat16),
            jax.ShapeDtypeStruct((18, 128), jnp.float32),
        ),
        in_specs=[VMEM, VMEM, VMEM, ANY],
        out_specs=(ANY, VMEM),
        scratch_shapes=[
            pltpu.VMEM((8, HID), jnp.float32),
            pltpu.VMEM((OWN, HID), jnp.float32),
            pltpu.VMEM((OWN, HID), jnp.bfloat16),
            pltpu.SemaphoreType.DMA((STRIPES,)),
            pltpu.SemaphoreType.DMA((STRIPES,)),
        ],
        compiler_params=pltpu.CompilerParams(vmem_limit_bytes=50 * MIB),
        name="update",
    )(spread(payload, DP), row_new, col_state.reshape(18, 128), grad)
    return (
        update.reshape(16, WID, HID),
        row_new.reshape(16, WID),
        col_new.reshape(HID),
    )


def solution(mesh):
    fine = Mesh(mesh.devices.reshape(8, 2, 4, 2, 2), ("z", "yl", "x", "yh", "core"))
    return jax.shard_map(
        body,
        mesh=fine,
        in_specs=(P(DP, MP), P(DP, MP), P(None, DP), P(MP)),
        out_specs=(P(None, DP, MP), P(None, DP), P(MP)),
        check_vma=False,
    )
```

```python
import functools

import jax
import jax.numpy as jnp
import numpy as np
from jax import lax
from jax.experimental import pallas as pl
from jax.experimental.pallas import tpu as pltpu
from jax.sharding import Mesh, PartitionSpec as P

D = 18432

decay = 1.0 - 2.0 ** (-0.8)
tiny = 1e-30

DP = ("z", "yl")
MP = ("x", "yh", "core")

TOK = 128
HID = 2304
WID = 72
OWN = 1152
ALL_TOK = 2048
FFW = 36864
CB = 256
BLOCKS = HID // CB
A_BLOCKS = 5
A_COLS = A_BLOCKS * CB
SPLIT = 4 * CB
A_UP = 3 * CB
EARLY = [(0, 0), (0, 1), (7, 0), (1, 0), (7, 1), (1, 1), (6, 0), (2, 0), (6, 1), (2, 1), (5, 0), (3, 0)]
LATE = [(5, 1), (3, 1), (4, 0), (4, 1)]
EARLY_TOK = len(EARLY) * TOK
LATE_TOK = len(LATE) * TOK
PLACES = np.array(
    [(EARLY + LATE).index((dz, dy)) for dz in range(8) for dy in range(2)], np.int32
)
MIB = 1024 * 1024
AHEAD = 3
LIMIT = 50 * MIB

ANY = pl.BlockSpec(memory_space=pl.ANY)
VMEM = pl.BlockSpec(memory_space=pltpu.VMEM)
SMEM = pl.BlockSpec(memory_space=pltpu.SMEM)


def ring(n, s):
    return [(i, (i + s) % n) for i in range(n)]


def send(v, axis, n, s):
    return lax.ppermute(v, axis, ring(n, s))


def tie(*v):
    return lax.optimization_barrier(v)


def up_z(v):
    return send(v, "z", 8, 1)


def down_z(v):
    return send(v, "z", 8, -1)


def other(v, axis):
    return send(v, axis, 2, 1)


def exchange(hidden, grad_out, pos):
    core = pos[4]

    def cross(*parts):
        return other(jnp.concatenate(parts, 0), "yl")

    def cut(v, first, last):
        return lax.slice_in_dim(v, first, last, axis=1)

    hidden, grad_out = tie(hidden, grad_out)
    u1, d1, near = up_z(hidden), down_z(hidden), other(hidden, "yl")
    turned = grad_out.T.reshape(16, WID, TOK)
    q = lax.all_to_all(turned, DP, 0, 0, tiled=True)
    u1, d1, near, q = tie(u1, d1, near, q)
    side = cut(near, 0, A_COLS)
    u2 = up_z(jnp.concatenate([u1, side], 1))
    d2 = down_z(jnp.concatenate([d1, side], 1))
    y1 = cross(cut(u1, A_COLS, HID), cut(d1, A_COLS, HID))
    keep = lax.dynamic_slice_in_dim(q, 8 * core, 8, 0)
    give = lax.dynamic_slice_in_dim(q, 8 - 8 * core, 8, 0)
    got = other(give, "core")
    first = jnp.where(core == 0, keep, got)
    second = jnp.where(core == 0, got, keep)
    half = jnp.concatenate([first, second], 1)
    far = other(half, "yh")
    f0, b0 = send(half, "x", 4, 1), send(half, "x", 4, -1)
    u2, d2, y1, far, f0, b0 = tie(u2, d2, y1, far, f0, b0)
    u3, d3 = up_z(u2), down_z(d2)
    y2 = cross(cut(u2, A_COLS, HID), cut(d2, A_COLS, HID))
    f1, b1 = send(far, "x", 4, 1), send(far, "x", 4, -1)
    o0 = send(f0, "x", 4, 1)
    o1 = send(b1, "x", 4, -1)
    mine = [half, f0, b0, o0, far, f1, b1, o1]
    theirs = [other(v, "core") for v in mine]
    u3, d3, y2, f1, o0, o1 = tie(u3, d3, y2, f1, o0, o1)
    u4 = up_z(jnp.concatenate([cut(u3, 0, SPLIT), cut(u3, HID, HID + A_COLS)], 1))
    d4 = down_z(cut(d3, SPLIT, HID + A_COLS))
    y3 = cross(cut(u3, A_COLS, HID), cut(d3, A_COLS, HID))
    features = mine + theirs
    n, m, h, k = BLOCKS, A_BLOCKS, SPLIT // CB, A_UP // CB
    pieces = [
        (hidden, 0, 0, 0, 0, 0, n),
        (near, 0, 0, 0, 1, 0, n),
        (u1, 0, 0, 7, 0, 0, n),
        (d1, 0, 0, 1, 0, 0, n),
        (y1, 0, -A_COLS, 7, 1, m, n),
        (y1, TOK, -A_COLS, 1, 1, m, n),
        (u2, 0, 0, 6, 0, 0, n),
        (d2, 0, 0, 2, 0, 0, n),
        (u2, 0, HID, 7, 1, 0, m),
        (d2, 0, HID, 1, 1, 0, m),
        (y2, 0, -A_COLS, 6, 1, m, n),
        (y2, TOK, -A_COLS, 2, 1, m, n),
        (u3, 0, 0, 5, 0, 0, n),
        (d3, 0, 0, 3, 0, 0, n),
        (u3, 0, HID, 6, 1, 0, m),
        (d3, 0, HID, 2, 1, 0, m),
    ]
    early, lhs = early_product(features, pieces, pos)
    u4, d4, y3, early = tie(u4, d4, y3, early)
    u5 = up_z(cut(u4, SPLIT, SPLIT + A_UP))
    d5 = down_z(cut(d4, HID - SPLIT + A_UP, HID - SPLIT + A_COLS))
    y4 = cross(cut(d4, A_COLS - SPLIT, HID - SPLIT))
    pieces = [
        (y3, 0, -A_COLS, 5, 1, m, n),
        (y3, TOK, -A_COLS, 3, 1, m, n),
        (u4, 0, 0, 4, 0, 0, h),
        (d4, 0, -SPLIT, 4, 0, h, n),
        (u4, 0, SPLIT, 5, 1, 0, m),
        (d4, 0, HID - SPLIT, 3, 1, 0, m),
        (y4, 0, -A_COLS, 4, 1, m, n),
        (u5, 0, 0, 4, 1, 0, k),
        (d5, 0, -A_UP, 4, 1, k, m),
    ]
    return late_product(lhs, early, pieces, pos)


def loader(plan, order, arrays, hid, hsem, z, yl):
    edges = sorted({p[5] for p in plan} | {p[6] for p in plan})

    def issue(j, slot):
        for lo, hi in zip(edges[:-1], edges[1:]):

            @pl.when((j >= lo) & (j < hi))
            def _(lo=lo):
                for index, row, base, dz, dy, first, last in plan:
                    if not first <= lo < last:
                        continue
                    col = pl.multiple_of(j * CB + base, CB)
                    place = order.index((dz, dy)) * TOK
                    pltpu.make_async_copy(
                        arrays[index].at[pl.ds(row, TOK), pl.ds(col, CB)],
                        hid.at[slot, place : place + TOK, :],
                        hsem.at[slot],
                    ).start()

    return issue


def column_block(grad, j):
    return grad.at[:, pl.ds(pl.multiple_of(j * CB, CB), CB)]


def early_kernel(plan, pos, places, *refs):
    features = refs[:16]
    arrays = refs[16:-25]
    grad, lhs_late = refs[-25:-23]
    stages = refs[-23:-7]
    lhs, hid, outbuf, fsem, lsem, hsem, osem = refs[-7:]
    z, yl, x, yh, core = pos[0], pos[1], pos[2], pos[3], pos[4]
    issue = loader(plan, EARLY, arrays, hid, hsem, z, yl)
    for k in range(16):
        pltpu.make_async_copy(features[k], stages[k], fsem.at[k]).start()
    issue(jnp.int32(0), 0)
    for k in range(16):
        pltpu.make_async_copy(features[k], stages[k], fsem.at[k]).wait()
        half = core if k < 8 else 1 - core
        dx, dy = (0, 3, 1, 2)[k % 4], (k // 4) % 2
        row = (lax.rem(x + dx, 4) * 2 + lax.rem(yh + dy, 2)) * (2 * WID)
        row = pl.multiple_of(row, 16)
        for i in range(8):
            s = half * 8 + i
            dz = lax.rem(s // 2 + 8 - z, 8)
            dy = lax.rem(lax.rem(s, 2) + 2 - yl, 2)
            col = pl.multiple_of(places[dz * 2 + dy] * TOK, TOK)
            lhs[pl.ds(row, 2 * WID), pl.ds(col, TOK)] = stages[k][i]
    late_copy = pltpu.make_async_copy(lhs.at[:, EARLY_TOK:], lhs_late, lsem)
    late_copy.start()

    def step(j, carry):
        slot = lax.rem(j, 2)

        @pl.when(j + 1 < BLOCKS)
        def _():
            issue(j + 1, 1 - slot)

        pltpu.make_async_copy(hid.at[slot], hid.at[slot], hsem.at[slot]).wait()

        @pl.when(j >= 2)
        def _():
            pltpu.make_async_copy(
                outbuf.at[slot], column_block(grad, j - 2), osem.at[slot]
            ).wait()

        for r in range(0, OWN, 384):
            outbuf[slot, r : r + 384, :] = jnp.dot(
                lhs[r : r + 384, :EARLY_TOK], hid[slot], preferred_element_type=jnp.float32
            )
        pltpu.make_async_copy(outbuf.at[slot], column_block(grad, j), osem.at[slot]).start()
        return carry

    lax.fori_loop(0, BLOCKS, step, 0)
    late_copy.wait()
    for j in range(BLOCKS - 2, BLOCKS):
        pltpu.make_async_copy(
            outbuf.at[j % 2], grad.at[:, j * CB : (j + 1) * CB], osem.at[j % 2]
        ).wait()


def numbered(pieces):
    arrays = []
    plan = []
    for piece in pieces:
        index = [i for i, a in enumerate(arrays) if a is piece[0]]
        if not index:
            arrays.append(piece[0])
            index = [len(arrays) - 1]
        plan.append((index[0],) + piece[1:])
    return arrays, plan


def early_product(features, pieces, pos):
    arrays, plan = numbered(pieces)
    return pl.pallas_call(
        functools.partial(early_kernel, plan),
        out_shape=(
            jax.ShapeDtypeStruct((OWN, HID), jnp.float32),
            jax.ShapeDtypeStruct((OWN, LATE_TOK), jnp.bfloat16),
        ),
        in_specs=[SMEM, SMEM] + [ANY] * (16 + len(arrays)),
        out_specs=(ANY, ANY),
        scratch_shapes=[pltpu.VMEM(v.shape, jnp.bfloat16) for v in features]
        + [
            pltpu.VMEM((OWN, ALL_TOK), jnp.bfloat16),
            pltpu.VMEM((2, EARLY_TOK, CB), jnp.bfloat16),
            pltpu.VMEM((2, OWN, CB), jnp.float32),
            pltpu.SemaphoreType.DMA((16,)),
            pltpu.SemaphoreType.DMA,
            pltpu.SemaphoreType.DMA((2,)),
            pltpu.SemaphoreType.DMA((2,)),
        ],
        compiler_params=pltpu.CompilerParams(vmem_limit_bytes=LIMIT),
        cost_estimate=pl.CostEstimate(
            flops=2 * OWN * HID * EARLY_TOK,
            bytes_accessed=OWN * HID * 4 + EARLY_TOK * HID * 2 + OWN * ALL_TOK * 2,
            transcendentals=0,
        ),
        name="early",
    )(pos, jnp.asarray(PLACES), *features, *arrays)


def late_kernel(plan, count, pos, lhs_hbm, before, *refs):
    arrays = refs[:count]
    grad, rows_out, cols_out = refs[count : count + 3]
    lhs, hid, whole, rowacc, lsem, hsem, bsem, osem = refs[count + 3 :]
    z, yl = pos[0], pos[1]
    issue = loader(plan, LATE, arrays, hid, hsem, z, yl)

    def block(j):
        return whole.at[:, pl.ds(pl.multiple_of(j * CB, CB), CB)]

    pltpu.make_async_copy(lhs_hbm, lhs, lsem).start()

    def fetch(j):
        issue(j, j)
        pltpu.make_async_copy(column_block(before, j), block(j), bsem.at[j]).start()

    for j in range(AHEAD):
        fetch(jnp.int32(j))
    rowacc[...] = jnp.zeros_like(rowacc)
    pltpu.make_async_copy(lhs_hbm, lhs, lsem).wait()

    def step(j, carry):
        @pl.when(j + AHEAD < BLOCKS)
        def _():
            fetch(j + AHEAD)

        pltpu.make_async_copy(hid.at[j], hid.at[j], hsem.at[j]).wait()
        pltpu.make_async_copy(column_block(before, j), block(j), bsem.at[j]).wait()
        cols = pl.ds(pl.multiple_of(j * CB, CB), CB)
        col = jnp.zeros((8, CB), jnp.float32)
        for r in range(0, OWN, 384):
            g = (
                jnp.dot(lhs[r : r + 384, :], hid[j], preferred_element_type=jnp.float32)
                + whole[r : r + 384, cols]
            ) * (1.0 / ALL_TOK)
            whole[r : r + 384, cols] = g
            sq = g * g
            rowacc[r : r + 384, :] += sq[:, :128] + sq[:, 128:]
            col = col + jnp.sum(sq.reshape(48, 8, CB), axis=0)
        total = jnp.sum(col, axis=0, keepdims=True)
        cols_out[pl.ds(2 * j, 1), :] = total[:, :128]
        cols_out[pl.ds(2 * j + 1, 1), :] = total[:, 128:]
        pltpu.make_async_copy(block(j), column_block(grad, j), osem.at[j]).start()
        return carry

    lax.fori_loop(0, BLOCKS, step, 0)
    for i in range(9):
        part = rowacc[i * 128 : (i + 1) * 128, :]
        line = jnp.sum(part.T, axis=0, keepdims=True)
        for d in range(16):
            rows_out[d, i : i + 1, :] = line
    for j in range(BLOCKS):
        pltpu.make_async_copy(
            block(jnp.int32(j)), column_block(grad, jnp.int32(j)), osem.at[j]
        ).wait()


def late_product(lhs, early, pieces, pos):
    arrays, plan = numbered(pieces)
    return pl.pallas_call(
        functools.partial(late_kernel, plan, len(arrays)),
        out_shape=(
            jax.ShapeDtypeStruct((OWN, HID), jnp.float32),
            jax.ShapeDtypeStruct((16, 9, 128), jnp.float32),
            jax.ShapeDtypeStruct((18, 128), jnp.float32),
        ),
        in_specs=[SMEM] + [ANY] * (2 + len(arrays)),
        out_specs=(ANY, VMEM, VMEM),
        scratch_shapes=[
            pltpu.VMEM((OWN, LATE_TOK), jnp.bfloat16),
            pltpu.VMEM((BLOCKS, LATE_TOK, CB), jnp.bfloat16),
            pltpu.VMEM((OWN, HID), jnp.float32),
            pltpu.VMEM((OWN, 128), jnp.float32),
            pltpu.SemaphoreType.DMA,
            pltpu.SemaphoreType.DMA((BLOCKS,)),
            pltpu.SemaphoreType.DMA((BLOCKS,)),
            pltpu.SemaphoreType.DMA((BLOCKS,)),
        ],
        compiler_params=pltpu.CompilerParams(vmem_limit_bytes=LIMIT),
        cost_estimate=pl.CostEstimate(
            flops=2 * OWN * HID * LATE_TOK,
            bytes_accessed=OWN * HID * 8 + LATE_TOK * HID * 2,
            transcendentals=0,
        ),
        name="late",
    )(pos, lhs, early, *arrays)


def middle_kernel(got, row_state, cols, row_new, payload):
    row_sum = jnp.sum(got[...], axis=0)
    new = decay * row_state[...] + (1.0 - decay) * (row_sum / FFW + tiny)
    row_new[...] = new
    total = jnp.sum(jnp.sum(new, axis=0, keepdims=True), axis=1, keepdims=True)
    for d in range(16):
        payload[d, :18, :] = cols[...]
        payload[d, 18:, :] = jnp.broadcast_to(total, (6, 128))


STRIPES = 9


def update_kernel(got, row_new, col_state, grad, out, col_new, colf, gbuf, obuf, rsem, wsem):
    def read(i):
        rows = pl.ds(i * 128, 128)
        return pltpu.make_async_copy(grad.at[rows, :], gbuf.at[rows, :], rsem.at[i])

    def write(i):
        rows = pl.ds(i * 128, 128)
        return pltpu.make_async_copy(obuf.at[rows, :], out.at[rows, :], wsem.at[i])

    for i in range(AHEAD):
        read(i).start()
    sums = jnp.sum(got[...], axis=0)
    new = decay * col_state[...] + (1.0 - decay) * (sums[:18, :] / D + tiny)
    col_new[...] = new
    inv = lax.rsqrt(new)
    for k in range(18):
        colf[:, k * 128 : (k + 1) * 128] = jnp.broadcast_to(inv[k : k + 1, :], (8, 128))
    scale = sums[18:19, :] / D
    rowf = lax.rsqrt(row_new[...]) * jnp.sqrt(scale)
    for i in range(STRIPES):
        if i + AHEAD < STRIPES:
            read(i + AHEAD).start()
        column = jnp.broadcast_to(rowf[i : i + 1, :], (128, 128)).T
        read(i).wait()
        for k in range(18):
            sl = slice(k * 128, (k + 1) * 128)
            obuf[i * 128 : (i + 1) * 128, sl] = (
                gbuf[i * 128 : (i + 1) * 128, sl] * (column * colf[0:1, sl])
            ).astype(jnp.bfloat16)
        write(i).start()
    for i in range(STRIPES):
        write(i).wait()


def spread(v, axes):
    return lax.all_to_all(v, axes, 0, 0, tiled=True)


def body(pre_act, grad_out, row_state, col_state):
    pos = jnp.stack([lax.axis_index(a) for a in ("z", "yl", "x", "yh", "core")]).astype(
        jnp.int32
    )
    hidden = jax.nn.gelu(pre_act.astype(jnp.float32)).astype(jnp.bfloat16)
    grad, rows, cols = exchange(hidden, grad_out, pos)
    row_new, payload = pl.pallas_call(
        middle_kernel,
        out_shape=(
            jax.ShapeDtypeStruct((9, 128), jnp.float32),
            jax.ShapeDtypeStruct((16, 24, 128), jnp.float32),
        ),
        in_specs=[VMEM] * 3,
        out_specs=(VMEM, VMEM),
        compiler_params=pltpu.CompilerParams(vmem_limit_bytes=4 * MIB),
        name="middle",
    )(spread(rows, MP), row_state.reshape(9, 128), cols)
    update, col_new = pl.pallas_call(
        update_kernel,
        out_shape=(
            jax.ShapeDtypeStruct((OWN, HID), jnp.bfloat16),
            jax.ShapeDtypeStruct((18, 128), jnp.float32),
        ),
        in_specs=[VMEM, VMEM, VMEM, ANY],
        out_specs=(ANY, VMEM),
        scratch_shapes=[
            pltpu.VMEM((8, HID), jnp.float32),
            pltpu.VMEM((OWN, HID), jnp.float32),
            pltpu.VMEM((OWN, HID), jnp.bfloat16),
            pltpu.SemaphoreType.DMA((STRIPES,)),
            pltpu.SemaphoreType.DMA((STRIPES,)),
        ],
        compiler_params=pltpu.CompilerParams(vmem_limit_bytes=LIMIT),
        name="update",
    )(spread(payload, DP), row_new, col_state.reshape(18, 128), grad)
    return (
        update.reshape(16, WID, HID),
        row_new.reshape(16, WID),
        col_new.reshape(HID),
    )


def solution(mesh):
    fine = Mesh(mesh.devices.reshape(8, 2, 4, 2, 2), ("z", "yl", "x", "yh", "core"))
    return jax.shard_map(
        body,
        mesh=fine,
        in_specs=(P(DP, MP), P(DP, MP), P(None, DP), P(MP)),
        out_specs=(P(None, DP, MP), P(None, DP), P(MP)),
        check_vma=False,
    )
```

```python
import functools

import jax
import jax.numpy as jnp
import numpy as np
from jax import lax
from jax.experimental import pallas as pl
from jax.experimental.pallas import tpu as pltpu
from jax.sharding import Mesh, PartitionSpec as P

D = 18432

decay = 1.0 - 2.0 ** (-0.8)
tiny = 1e-30

DP = ("z", "yl")
MP = ("x", "yh", "core")

TOK = 128
HID = 2304
WID = 72
OWN = 1152
ALL_TOK = 2048
FFW = 36864
CB = 256
BLOCKS = HID // CB
A_BLOCKS = 5
A_COLS = A_BLOCKS * CB
B_COLS = HID - A_COLS
SPLIT = 4 * CB
A_UP = 3 * CB
EARLY = [(0, 0), (0, 1), (7, 0), (1, 0), (7, 1), (1, 1), (6, 0), (2, 0), (6, 1), (2, 1), (5, 0), (3, 0)]
LATE = [(5, 1), (3, 1), (4, 0), (4, 1)]
EARLY_TOK = len(EARLY) * TOK
LATE_TOK = len(LATE) * TOK
PLACES = np.array(
    [(EARLY + LATE).index((dz, dy)) for dz in range(8) for dy in range(2)], np.int32
)
MIB = 1024 * 1024
AHEAD = 5
LIMIT = 50 * MIB

ANY = pl.BlockSpec(memory_space=pl.ANY)
VMEM = pl.BlockSpec(memory_space=pltpu.VMEM)
SMEM = pl.BlockSpec(memory_space=pltpu.SMEM)


def ring(n, s):
    return [(i, (i + s) % n) for i in range(n)]


def send(v, axis, n, s):
    return lax.ppermute(v, axis, ring(n, s))


def tie(*v):
    return lax.optimization_barrier(v)


def up_z(v):
    return send(v, "z", 8, 1)


def down_z(v):
    return send(v, "z", 8, -1)


def other(v, axis):
    return send(v, axis, 2, 1)


def pack_kernel(plan, *refs):
    for source, row, first, target, at_row, at, width in plan:
        refs[target][at_row : at_row + TOK, at : at + width] = refs[source][
            row : row + TOK, first : first + width
        ]


def pack(sources, shapes, plan):
    n = len(sources)
    return pl.pallas_call(
        functools.partial(pack_kernel, [p[:3] + (p[3] + n,) + p[4:] for p in plan]),
        out_shape=[jax.ShapeDtypeStruct(v, jnp.bfloat16) for v in shapes],
        in_specs=[VMEM] * n,
        out_specs=[VMEM] * len(shapes),
        compiler_params=pltpu.CompilerParams(vmem_limit_bytes=8 * MIB),
        cost_estimate=pl.CostEstimate(flops=0, bytes_accessed=4 * MIB, transcendentals=0),
        name="pack",
    )(*sources)


def exchange(hidden, grad_out, pos):
    core = pos[4]

    def cross(*parts):
        return other(jnp.concatenate(parts, 0), "yl")

    def cut(v, first, last):
        return lax.slice_in_dim(v, first, last, axis=1)

    hidden, grad_out = tie(hidden, grad_out)
    u1, d1, near = up_z(hidden), down_z(hidden), other(hidden, "yl")
    turned = grad_out.T.reshape(16, WID, TOK)
    q = lax.all_to_all(turned, DP, 0, 0, tiled=True)
    u1, d1, near, q = tie(u1, d1, near, q)
    side = cut(near, 0, A_COLS)
    u2 = up_z(jnp.concatenate([u1, side], 1))
    d2 = down_z(jnp.concatenate([d1, side], 1))
    y1 = cross(cut(u1, A_COLS, HID), cut(d1, A_COLS, HID))
    keep = lax.dynamic_slice_in_dim(q, 8 * core, 8, 0)
    give = lax.dynamic_slice_in_dim(q, 8 - 8 * core, 8, 0)
    got = other(give, "core")
    first = jnp.where(core == 0, keep, got)
    second = jnp.where(core == 0, got, keep)
    half = jnp.concatenate([first, second], 1)
    far = other(half, "yh")
    f0, b0 = send(half, "x", 4, 1), send(half, "x", 4, -1)
    u2, d2, y1, far, f0, b0 = tie(u2, d2, y1, far, f0, b0)
    u3, d3 = up_z(u2), down_z(d2)
    y2 = cross(cut(u2, A_COLS, HID), cut(d2, A_COLS, HID))
    f1, b1 = send(far, "x", 4, 1), send(far, "x", 4, -1)
    o0 = send(f0, "x", 4, 1)
    o1 = send(b1, "x", 4, -1)
    mine = [half, f0, b0, o0, far, f1, b1, o1]
    theirs = [other(v, "core") for v in mine]
    u3, d3, y2, f1, o0, o1 = tie(u3, d3, y2, f1, o0, o1)
    m3, mu, md = pack(
        [u3, d3],
        [(2 * TOK, B_COLS), (TOK, SPLIT + A_COLS), (TOK, HID - SPLIT + A_COLS)],
        [
            (0, 0, A_COLS, 0, 0, 0, B_COLS),
            (1, 0, A_COLS, 0, TOK, 0, B_COLS),
            (0, 0, 0, 1, 0, 0, SPLIT),
            (0, 0, HID, 1, 0, SPLIT, A_COLS),
            (1, 0, SPLIT, 2, 0, 0, HID - SPLIT + A_COLS),
        ],
    )
    u4, d4, y3 = up_z(mu), down_z(md), other(m3, "yl")
    features = mine + theirs
    n, m, h, k = BLOCKS, A_BLOCKS, SPLIT // CB, A_UP // CB
    pieces = [
        (hidden, 0, 0, 0, 0, 0, n),
        (near, 0, 0, 0, 1, 0, n),
        (u1, 0, 0, 7, 0, 0, n),
        (d1, 0, 0, 1, 0, 0, n),
        (y1, 0, -A_COLS, 7, 1, m, n),
        (y1, TOK, -A_COLS, 1, 1, m, n),
        (u2, 0, 0, 6, 0, 0, n),
        (d2, 0, 0, 2, 0, 0, n),
        (u2, 0, HID, 7, 1, 0, m),
        (d2, 0, HID, 1, 1, 0, m),
        (y2, 0, -A_COLS, 6, 1, m, n),
        (y2, TOK, -A_COLS, 2, 1, m, n),
        (u3, 0, 0, 5, 0, 0, n),
        (d3, 0, 0, 3, 0, 0, n),
        (u3, 0, HID, 6, 1, 0, m),
        (d3, 0, HID, 2, 1, 0, m),
    ]
    early, lhs = early_product(features, pieces, pos)
    u4, d4, y3, early = tie(u4, d4, y3, early)
    u5 = up_z(cut(u4, SPLIT, SPLIT + A_UP))
    d5 = down_z(cut(d4, HID - SPLIT + A_UP, HID - SPLIT + A_COLS))
    y4 = cross(cut(d4, A_COLS - SPLIT, HID - SPLIT))
    pieces = [
        (y3, 0, -A_COLS, 5, 1, m, n),
        (y3, TOK, -A_COLS, 3, 1, m, n),
        (u4, 0, 0, 4, 0, 0, h),
        (d4, 0, -SPLIT, 4, 0, h, n),
        (u4, 0, SPLIT, 5, 1, 0, m),
        (d4, 0, HID - SPLIT, 3, 1, 0, m),
        (y4, 0, -A_COLS, 4, 1, m, n),
        (u5, 0, 0, 4, 1, 0, k),
        (d5, 0, -A_UP, 4, 1, k, m),
    ]
    return late_product(lhs, early, pieces, pos)


def loader(plan, order, arrays, hid, hsem, z, yl):
    edges = sorted({p[5] for p in plan} | {p[6] for p in plan})

    def issue(j, slot):
        for lo, hi in zip(edges[:-1], edges[1:]):

            @pl.when((j >= lo) & (j < hi))
            def _(lo=lo):
                for index, row, base, dz, dy, first, last in plan:
                    if not first <= lo < last:
                        continue
                    col = pl.multiple_of(j * CB + base, CB)
                    place = order.index((dz, dy)) * TOK
                    pltpu.make_async_copy(
                        arrays[index].at[pl.ds(row, TOK), pl.ds(col, CB)],
                        hid.at[slot, place : place + TOK, :],
                        hsem.at[slot],
                    ).start()

    return issue


def column_block(grad, j):
    return grad.at[:, pl.ds(pl.multiple_of(j * CB, CB), CB)]


def early_kernel(plan, pos, places, *refs):
    features = refs[:16]
    arrays = refs[16:-25]
    grad, lhs_late = refs[-25:-23]
    stages = refs[-23:-7]
    lhs, hid, outbuf, fsem, lsem, hsem, osem = refs[-7:]
    z, yl, x, yh, core = pos[0], pos[1], pos[2], pos[3], pos[4]
    issue = loader(plan, EARLY, arrays, hid, hsem, z, yl)
    for k in range(16):
        pltpu.make_async_copy(features[k], stages[k], fsem.at[k]).start()
    issue(jnp.int32(0), 0)
    for k in range(16):
        pltpu.make_async_copy(features[k], stages[k], fsem.at[k]).wait()
        half = core if k < 8 else 1 - core
        dx, dy = (0, 3, 1, 2)[k % 4], (k // 4) % 2
        row = (lax.rem(x + dx, 4) * 2 + lax.rem(yh + dy, 2)) * (2 * WID)
        row = pl.multiple_of(row, 16)
        for i in range(8):
            s = half * 8 + i
            dz = lax.rem(s // 2 + 8 - z, 8)
            dy = lax.rem(lax.rem(s, 2) + 2 - yl, 2)
            col = pl.multiple_of(places[dz * 2 + dy] * TOK, TOK)
            lhs[pl.ds(row, 2 * WID), pl.ds(col, TOK)] = stages[k][i]
    late_copy = pltpu.make_async_copy(lhs.at[:, EARLY_TOK:], lhs_late, lsem)
    late_copy.start()

    def step(j, carry):
        slot = lax.rem(j, 2)

        @pl.when(j + 1 < BLOCKS)
        def _():
            issue(j + 1, 1 - slot)

        pltpu.make_async_copy(hid.at[slot], hid.at[slot], hsem.at[slot]).wait()

        @pl.when(j >= 2)
        def _():
            pltpu.make_async_copy(
                outbuf.at[slot], column_block(grad, j - 2), osem.at[slot]
            ).wait()

        for r in range(0, OWN, 384):
            outbuf[slot, r : r + 384, :] = jnp.dot(
                lhs[r : r + 384, :EARLY_TOK], hid[slot], preferred_element_type=jnp.float32
            )
        pltpu.make_async_copy(outbuf.at[slot], column_block(grad, j), osem.at[slot]).start()
        return carry

    lax.fori_loop(0, BLOCKS, step, 0)
    late_copy.wait()
    for j in range(BLOCKS - 2, BLOCKS):
        pltpu.make_async_copy(
            outbuf.at[j % 2], grad.at[:, j * CB : (j + 1) * CB], osem.at[j % 2]
        ).wait()


def numbered(pieces):
    arrays = []
    plan = []
    for piece in pieces:
        index = [i for i, a in enumerate(arrays) if a is piece[0]]
        if not index:
            arrays.append(piece[0])
            index = [len(arrays) - 1]
        plan.append((index[0],) + piece[1:])
    return arrays, plan


def early_product(features, pieces, pos):
    arrays, plan = numbered(pieces)
    return pl.pallas_call(
        functools.partial(early_kernel, plan),
        out_shape=(
            jax.ShapeDtypeStruct((OWN, HID), jnp.float32),
            jax.ShapeDtypeStruct((OWN, LATE_TOK), jnp.bfloat16),
        ),
        in_specs=[SMEM, SMEM] + [ANY] * (16 + len(arrays)),
        out_specs=(ANY, ANY),
        scratch_shapes=[pltpu.VMEM(v.shape, jnp.bfloat16) for v in features]
        + [
            pltpu.VMEM((OWN, ALL_TOK), jnp.bfloat16),
            pltpu.VMEM((2, EARLY_TOK, CB), jnp.bfloat16),
            pltpu.VMEM((2, OWN, CB), jnp.float32),
            pltpu.SemaphoreType.DMA((16,)),
            pltpu.SemaphoreType.DMA,
            pltpu.SemaphoreType.DMA((2,)),
            pltpu.SemaphoreType.DMA((2,)),
        ],
        compiler_params=pltpu.CompilerParams(vmem_limit_bytes=LIMIT),
        cost_estimate=pl.CostEstimate(
            flops=2 * OWN * HID * EARLY_TOK,
            bytes_accessed=OWN * HID * 4 + EARLY_TOK * HID * 2 + OWN * ALL_TOK * 2,
            transcendentals=0,
        ),
        name="early",
    )(pos, jnp.asarray(PLACES), *features, *arrays)


def late_kernel(plan, count, pos, lhs_hbm, before, *refs):
    arrays = refs[:count]
    grad, rows_out, cols_out = refs[count : count + 3]
    lhs, hid, whole, rowacc, lsem, hsem, bsem, osem = refs[count + 3 :]
    z, yl = pos[0], pos[1]
    issue = loader(plan, LATE, arrays, hid, hsem, z, yl)

    def block(j):
        return whole.at[:, pl.ds(pl.multiple_of(j * CB, CB), CB)]

    pltpu.make_async_copy(lhs_hbm, lhs, lsem).start()

    def fetch(j):
        issue(j, j)
        pltpu.make_async_copy(column_block(before, j), block(j), bsem.at[j]).start()

    for j in range(AHEAD):
        fetch(jnp.int32(j))
    rowacc[...] = jnp.zeros_like(rowacc)
    pltpu.make_async_copy(lhs_hbm, lhs, lsem).wait()

    def step(j, carry):
        @pl.when(j + AHEAD < BLOCKS)
        def _():
            fetch(j + AHEAD)

        pltpu.make_async_copy(hid.at[j], hid.at[j], hsem.at[j]).wait()
        pltpu.make_async_copy(column_block(before, j), block(j), bsem.at[j]).wait()
        cols = pl.ds(pl.multiple_of(j * CB, CB), CB)
        col = jnp.zeros((8, CB), jnp.float32)
        for r in range(0, OWN, 384):
            g = (
                jnp.dot(lhs[r : r + 384, :], hid[j], preferred_element_type=jnp.float32)
                + whole[r : r + 384, cols]
            ) * (1.0 / ALL_TOK)
            whole[r : r + 384, cols] = g
            sq = g * g
            rowacc[r : r + 384, :] += sq[:, :128] + sq[:, 128:]
            col = col + jnp.sum(sq.reshape(48, 8, CB), axis=0)
        total = jnp.sum(col, axis=0, keepdims=True)
        cols_out[pl.ds(2 * j, 1), :] = total[:, :128]
        cols_out[pl.ds(2 * j + 1, 1), :] = total[:, 128:]
        pltpu.make_async_copy(block(j), column_block(grad, j), osem.at[j]).start()
        return carry

    lax.fori_loop(0, BLOCKS, step, 0)
    for i in range(9):
        part = rowacc[i * 128 : (i + 1) * 128, :]
        line = jnp.sum(part.T, axis=0, keepdims=True)
        for d in range(16):
            rows_out[d, i : i + 1, :] = line
    for j in range(BLOCKS):
        pltpu.make_async_copy(
            block(jnp.int32(j)), column_block(grad, jnp.int32(j)), osem.at[j]
        ).wait()


def late_product(lhs, early, pieces, pos):
    arrays, plan = numbered(pieces)
    return pl.pallas_call(
        functools.partial(late_kernel, plan, len(arrays)),
        out_shape=(
            jax.ShapeDtypeStruct((OWN, HID), jnp.float32),
            jax.ShapeDtypeStruct((16, 9, 128), jnp.float32),
            jax.ShapeDtypeStruct((18, 128), jnp.float32),
        ),
        in_specs=[SMEM] + [ANY] * (2 + len(arrays)),
        out_specs=(ANY, VMEM, VMEM),
        scratch_shapes=[
            pltpu.VMEM((OWN, LATE_TOK), jnp.bfloat16),
            pltpu.VMEM((BLOCKS, LATE_TOK, CB), jnp.bfloat16),
            pltpu.VMEM((OWN, HID), jnp.float32),
            pltpu.VMEM((OWN, 128), jnp.float32),
            pltpu.SemaphoreType.DMA,
            pltpu.SemaphoreType.DMA((BLOCKS,)),
            pltpu.SemaphoreType.DMA((BLOCKS,)),
            pltpu.SemaphoreType.DMA((BLOCKS,)),
        ],
        compiler_params=pltpu.CompilerParams(vmem_limit_bytes=LIMIT),
        cost_estimate=pl.CostEstimate(
            flops=2 * OWN * HID * LATE_TOK,
            bytes_accessed=OWN * HID * 8 + LATE_TOK * HID * 2,
            transcendentals=0,
        ),
        name="late",
    )(pos, lhs, early, *arrays)


def middle_kernel(got, row_state, cols, row_new, payload):
    row_sum = jnp.sum(got[...], axis=0)
    new = decay * row_state[...] + (1.0 - decay) * (row_sum / FFW + tiny)
    row_new[...] = new
    total = jnp.sum(jnp.sum(new, axis=0, keepdims=True), axis=1, keepdims=True)
    for d in range(16):
        payload[d, :18, :] = cols[...]
        payload[d, 18:, :] = jnp.broadcast_to(total, (6, 128))


STRIPES = 9


def update_kernel(got, row_new, col_state, grad, out, col_new, colf, gbuf, obuf, rsem, wsem):
    def read(i):
        rows = pl.ds(i * 128, 128)
        return pltpu.make_async_copy(grad.at[rows, :], gbuf.at[rows, :], rsem.at[i])

    def write(i):
        rows = pl.ds(i * 128, 128)
        return pltpu.make_async_copy(obuf.at[rows, :], out.at[rows, :], wsem.at[i])

    for i in range(AHEAD):
        read(i).start()
    sums = jnp.sum(got[...], axis=0)
    new = decay * col_state[...] + (1.0 - decay) * (sums[:18, :] / D + tiny)
    col_new[...] = new
    inv = lax.rsqrt(new)
    for k in range(18):
        colf[:, k * 128 : (k + 1) * 128] = jnp.broadcast_to(inv[k : k + 1, :], (8, 128))
    scale = sums[18:19, :] / D
    rowf = lax.rsqrt(row_new[...]) * jnp.sqrt(scale)
    for i in range(STRIPES):
        if i + AHEAD < STRIPES:
            read(i + AHEAD).start()
        column = jnp.broadcast_to(rowf[i : i + 1, :], (128, 128)).T
        read(i).wait()
        for k in range(18):
            sl = slice(k * 128, (k + 1) * 128)
            obuf[i * 128 : (i + 1) * 128, sl] = (
                gbuf[i * 128 : (i + 1) * 128, sl] * (column * colf[0:1, sl])
            ).astype(jnp.bfloat16)
        write(i).start()
    for i in range(STRIPES):
        write(i).wait()


def spread(v, axes):
    return lax.all_to_all(v, axes, 0, 0, tiled=True)


def body(pre_act, grad_out, row_state, col_state):
    pos = jnp.stack([lax.axis_index(a) for a in ("z", "yl", "x", "yh", "core")]).astype(
        jnp.int32
    )
    hidden = jax.nn.gelu(pre_act.astype(jnp.float32)).astype(jnp.bfloat16)
    grad, rows, cols = exchange(hidden, grad_out, pos)
    row_new, payload = pl.pallas_call(
        middle_kernel,
        out_shape=(
            jax.ShapeDtypeStruct((9, 128), jnp.float32),
            jax.ShapeDtypeStruct((16, 24, 128), jnp.float32),
        ),
        in_specs=[VMEM] * 3,
        out_specs=(VMEM, VMEM),
        compiler_params=pltpu.CompilerParams(vmem_limit_bytes=4 * MIB),
        name="middle",
    )(spread(rows, MP), row_state.reshape(9, 128), cols)
    update, col_new = pl.pallas_call(
        update_kernel,
        out_shape=(
            jax.ShapeDtypeStruct((OWN, HID), jnp.bfloat16),
            jax.ShapeDtypeStruct((18, 128), jnp.float32),
        ),
        in_specs=[VMEM, VMEM, VMEM, ANY],
        out_specs=(ANY, VMEM),
        scratch_shapes=[
            pltpu.VMEM((8, HID), jnp.float32),
            pltpu.VMEM((OWN, HID), jnp.float32),
            pltpu.VMEM((OWN, HID), jnp.bfloat16),
            pltpu.SemaphoreType.DMA((STRIPES,)),
            pltpu.SemaphoreType.DMA((STRIPES,)),
        ],
        compiler_params=pltpu.CompilerParams(vmem_limit_bytes=LIMIT),
        name="update",
    )(spread(payload, DP), row_new, col_state.reshape(18, 128), grad)
    return (
        update.reshape(16, WID, HID),
        row_new.reshape(16, WID),
        col_new.reshape(HID),
    )


def solution(mesh):
    fine = Mesh(mesh.devices.reshape(8, 2, 4, 2, 2), ("z", "yl", "x", "yh", "core"))
    return jax.shard_map(
        body,
        mesh=fine,
        in_specs=(P(DP, MP), P(DP, MP), P(None, DP), P(MP)),
        out_specs=(P(None, DP, MP), P(None, DP), P(MP)),
        check_vma=False,
    )
```

```python
import functools

import jax
import jax.numpy as jnp
import numpy as np
from jax import lax
from jax.experimental import pallas as pl
from jax.experimental.pallas import tpu as pltpu
from jax.sharding import Mesh, PartitionSpec as P

D = 18432

decay = 1.0 - 2.0 ** (-0.8)
tiny = 1e-30

DP = ("z", "yl")
MP = ("x", "yh", "core")

TOK = 128
HID = 2304
WID = 72
OWN = 1152
ALL_TOK = 2048
FFW = 36864
CB = 256
BLOCKS = HID // CB
A_BLOCKS = 5
A_COLS = A_BLOCKS * CB
B_COLS = HID - A_COLS
SPLIT = 4 * CB
A_UP = 3 * CB
EARLY = [(0, 0), (0, 1), (7, 0), (1, 0), (7, 1), (1, 1), (6, 0), (2, 0), (6, 1), (2, 1), (5, 0), (3, 0)]
LATE = [(5, 1), (3, 1), (4, 0), (4, 1)]
EARLY_TOK = len(EARLY) * TOK
LATE_TOK = len(LATE) * TOK
PLACES = np.array(
    [(EARLY + LATE).index((dz, dy)) for dz in range(8) for dy in range(2)], np.int32
)
MIB = 1024 * 1024
AHEAD = 5
LIMIT = 50 * MIB

ANY = pl.BlockSpec(memory_space=pl.ANY)
VMEM = pl.BlockSpec(memory_space=pltpu.VMEM)
SMEM = pl.BlockSpec(memory_space=pltpu.SMEM)


def ring(n, s):
    return [(i, (i + s) % n) for i in range(n)]


def send(v, axis, n, s):
    return lax.ppermute(v, axis, ring(n, s))


def tie(*v):
    return lax.optimization_barrier(v)


def up_z(v):
    return send(v, "z", 8, 1)


def down_z(v):
    return send(v, "z", 8, -1)


def other(v, axis):
    return send(v, axis, 2, 1)


def pack_kernel(plan, *refs):
    for source, row, first, target, at_row, at, width in plan:
        refs[target][at_row : at_row + TOK, at : at + width] = refs[source][
            row : row + TOK, first : first + width
        ]


def pack(sources, shapes, plan):
    n = len(sources)
    return pl.pallas_call(
        functools.partial(pack_kernel, [p[:3] + (p[3] + n,) + p[4:] for p in plan]),
        out_shape=[jax.ShapeDtypeStruct(v, jnp.bfloat16) for v in shapes],
        in_specs=[VMEM] * n,
        out_specs=[VMEM] * len(shapes),
        compiler_params=pltpu.CompilerParams(vmem_limit_bytes=8 * MIB),
        cost_estimate=pl.CostEstimate(flops=0, bytes_accessed=4 * MIB, transcendentals=0),
        name="pack",
    )(*sources)


def exchange(hidden, grad_out, pos):
    core = pos[4]

    def cross(*parts):
        return other(jnp.concatenate(parts, 0), "yl")

    def cut(v, first, last):
        return lax.slice_in_dim(v, first, last, axis=1)

    hidden, grad_out = tie(hidden, grad_out)
    u1, d1, near = up_z(hidden), down_z(hidden), other(hidden, "yl")
    turned = grad_out.T.reshape(16, WID, TOK)
    q = lax.all_to_all(turned, DP, 0, 0, tiled=True)
    u1, d1, near, q = tie(u1, d1, near, q)
    side = cut(near, 0, A_COLS)
    u2 = up_z(jnp.concatenate([u1, side], 1))
    d2 = down_z(jnp.concatenate([d1, side], 1))
    y1 = cross(cut(u1, A_COLS, HID), cut(d1, A_COLS, HID))
    keep = lax.dynamic_slice_in_dim(q, 8 * core, 8, 0)
    give = lax.dynamic_slice_in_dim(q, 8 - 8 * core, 8, 0)
    got = other(give, "core")
    first = jnp.where(core == 0, keep, got)
    second = jnp.where(core == 0, got, keep)
    half = jnp.concatenate([first, second], 1)
    far = other(half, "yh")
    f0, b0 = send(half, "x", 4, 1), send(half, "x", 4, -1)
    u2, d2, y1, far, f0, b0 = tie(u2, d2, y1, far, f0, b0)
    u3, d3 = up_z(u2), down_z(d2)
    y2 = cross(cut(u2, A_COLS, HID), cut(d2, A_COLS, HID))
    f1, b1 = send(far, "x", 4, 1), send(far, "x", 4, -1)
    o0 = send(f0, "x", 4, 1)
    o1 = send(b1, "x", 4, -1)
    mine = [half, f0, b0, o0, far, f1, b1, o1]
    theirs = [other(v, "core") for v in mine]
    u3, d3, y2, f1, o0, o1 = tie(u3, d3, y2, f1, o0, o1)
    m3, mu, md = pack(
        [u3, d3],
        [(2 * TOK, B_COLS), (TOK, SPLIT + A_COLS), (TOK, HID - SPLIT + A_COLS)],
        [
            (0, 0, A_COLS, 0, 0, 0, B_COLS),
            (1, 0, A_COLS, 0, TOK, 0, B_COLS),
            (0, 0, 0, 1, 0, 0, SPLIT),
            (0, 0, HID, 1, 0, SPLIT, A_COLS),
            (1, 0, SPLIT, 2, 0, 0, HID - SPLIT + A_COLS),
        ],
    )
    u4, d4, y3 = up_z(mu), down_z(md), other(m3, "yl")
    features = mine + theirs
    n, m, h, k = BLOCKS, A_BLOCKS, SPLIT // CB, A_UP // CB
    pieces = [
        (hidden, 0, 0, 0, 0, 0, n),
        (near, 0, 0, 0, 1, 0, n),
        (u1, 0, 0, 7, 0, 0, n),
        (d1, 0, 0, 1, 0, 0, n),
        (y1, 0, -A_COLS, 7, 1, m, n),
        (y1, TOK, -A_COLS, 1, 1, m, n),
        (u2, 0, 0, 6, 0, 0, n),
        (d2, 0, 0, 2, 0, 0, n),
        (u2, 0, HID, 7, 1, 0, m),
        (d2, 0, HID, 1, 1, 0, m),
        (y2, 0, -A_COLS, 6, 1, m, n),
        (y2, TOK, -A_COLS, 2, 1, m, n),
        (u3, 0, 0, 5, 0, 0, n),
        (d3, 0, 0, 3, 0, 0, n),
        (u3, 0, HID, 6, 1, 0, m),
        (d3, 0, HID, 2, 1, 0, m),
    ]
    early, lhs = early_product(features, pieces, pos)
    u4, d4, y3, early = tie(u4, d4, y3, early)
    u5 = up_z(cut(u4, SPLIT, SPLIT + A_UP))
    d5 = down_z(cut(d4, HID - SPLIT + A_UP, HID - SPLIT + A_COLS))
    y4 = cross(cut(d4, A_COLS - SPLIT, HID - SPLIT))
    pieces = [
        (y3, 0, -A_COLS, 5, 1, m, n),
        (y3, TOK, -A_COLS, 3, 1, m, n),
        (u4, 0, 0, 4, 0, 0, h),
        (d4, 0, -SPLIT, 4, 0, h, n),
        (u4, 0, SPLIT, 5, 1, 0, m),
        (d4, 0, HID - SPLIT, 3, 1, 0, m),
        (y4, 0, -A_COLS, 4, 1, m, n),
        (u5, 0, 0, 4, 1, 0, k),
        (d5, 0, -A_UP, 4, 1, k, m),
    ]
    return late_product(lhs, early, pieces, pos)


def loader(plan, order, arrays, hid, hsem, z, yl):
    edges = sorted({p[5] for p in plan} | {p[6] for p in plan})

    def issue(j, slot):
        for lo, hi in zip(edges[:-1], edges[1:]):

            @pl.when((j >= lo) & (j < hi))
            def _(lo=lo):
                for index, row, base, dz, dy, first, last in plan:
                    if not first <= lo < last:
                        continue
                    col = pl.multiple_of(j * CB + base, CB)
                    place = order.index((dz, dy)) * TOK
                    pltpu.make_async_copy(
                        arrays[index].at[pl.ds(row, TOK), pl.ds(col, CB)],
                        hid.at[slot, place : place + TOK, :],
                        hsem.at[slot],
                    ).start()

    return issue


def column_block(grad, j):
    return grad.at[:, pl.ds(pl.multiple_of(j * CB, CB), CB)]


def early_kernel(plan, pos, places, *refs):
    features = refs[:16]
    arrays = refs[16:-25]
    grad, lhs_late = refs[-25:-23]
    stages = refs[-23:-7]
    lhs, hid, outbuf, fsem, lsem, hsem, osem = refs[-7:]
    z, yl, x, yh, core = pos[0], pos[1], pos[2], pos[3], pos[4]
    issue = loader(plan, EARLY, arrays, hid, hsem, z, yl)
    for k in range(16):
        pltpu.make_async_copy(features[k], stages[k], fsem.at[k]).start()
    issue(jnp.int32(0), 0)
    cols = []
    for half in (core, 1 - core):
        for i in range(8):
            dz = lax.rem(half * 4 + (8 + i // 2) - z, 8)
            dy = lax.rem((2 + i % 2) - yl, 2)
            cols.append(pl.multiple_of(places[dz * 2 + dy] * TOK, TOK))
    for k in range(16):
        dx, dy = (0, 3, 1, 2)[k % 4], (k // 4) % 2
        row = (lax.rem(x + dx, 4) * 2 + lax.rem(yh + dy, 2)) * (2 * WID)
        row = pl.multiple_of(row, 16)
        pltpu.make_async_copy(features[k], stages[k], fsem.at[k]).wait()
        for i in range(8):
            col = cols[k // 8 * 8 + i]
            lhs[pl.ds(row, 2 * WID), pl.ds(col, TOK)] = stages[k][i]
    late_copy = pltpu.make_async_copy(lhs.at[:, EARLY_TOK:], lhs_late, lsem)
    late_copy.start()

    def step(j, carry):
        slot = lax.rem(j, 2)

        @pl.when(j + 1 < BLOCKS)
        def _():
            issue(j + 1, 1 - slot)

        pltpu.make_async_copy(hid.at[slot], hid.at[slot], hsem.at[slot]).wait()

        @pl.when(j >= 2)
        def _():
            pltpu.make_async_copy(
                outbuf.at[slot], column_block(grad, j - 2), osem.at[slot]
            ).wait()

        for r in range(0, OWN, 384):
            outbuf[slot, r : r + 384, :] = jnp.dot(
                lhs[r : r + 384, :EARLY_TOK], hid[slot], preferred_element_type=jnp.float32
            )
        pltpu.make_async_copy(outbuf.at[slot], column_block(grad, j), osem.at[slot]).start()
        return carry

    lax.fori_loop(0, BLOCKS, step, 0)
    late_copy.wait()
    for j in range(BLOCKS - 2, BLOCKS):
        pltpu.make_async_copy(
            outbuf.at[j % 2], grad.at[:, j * CB : (j + 1) * CB], osem.at[j % 2]
        ).wait()


def numbered(pieces):
    arrays = []
    plan = []
    for piece in pieces:
        index = [i for i, a in enumerate(arrays) if a is piece[0]]
        if not index:
            arrays.append(piece[0])
            index = [len(arrays) - 1]
        plan.append((index[0],) + piece[1:])
    return arrays, plan


def early_product(features, pieces, pos):
    arrays, plan = numbered(pieces)
    return pl.pallas_call(
        functools.partial(early_kernel, plan),
        out_shape=(
            jax.ShapeDtypeStruct((OWN, HID), jnp.float32),
            jax.ShapeDtypeStruct((OWN, LATE_TOK), jnp.bfloat16),
        ),
        in_specs=[SMEM, SMEM] + [ANY] * (16 + len(arrays)),
        out_specs=(ANY, ANY),
        scratch_shapes=[pltpu.VMEM(v.shape, jnp.bfloat16) for v in features]
        + [
            pltpu.VMEM((OWN, ALL_TOK), jnp.bfloat16),
            pltpu.VMEM((2, EARLY_TOK, CB), jnp.bfloat16),
            pltpu.VMEM((2, OWN, CB), jnp.float32),
            pltpu.SemaphoreType.DMA((16,)),
            pltpu.SemaphoreType.DMA,
            pltpu.SemaphoreType.DMA((2,)),
            pltpu.SemaphoreType.DMA((2,)),
        ],
        compiler_params=pltpu.CompilerParams(vmem_limit_bytes=LIMIT),
        cost_estimate=pl.CostEstimate(
            flops=2 * OWN * HID * EARLY_TOK,
            bytes_accessed=OWN * HID * 4 + EARLY_TOK * HID * 2 + OWN * ALL_TOK * 2,
            transcendentals=0,
        ),
        name="early",
    )(pos, jnp.asarray(PLACES), *features, *arrays)


def late_kernel(plan, count, pos, lhs_hbm, before, *refs):
    arrays = refs[:count]
    grad, rows_out, cols_out = refs[count : count + 3]
    lhs, hid, whole, rowacc, lsem, hsem, bsem, osem = refs[count + 3 :]
    z, yl = pos[0], pos[1]
    issue = loader(plan, LATE, arrays, hid, hsem, z, yl)

    def block(j):
        return whole.at[:, pl.ds(pl.multiple_of(j * CB, CB), CB)]

    pltpu.make_async_copy(lhs_hbm, lhs, lsem).start()

    def fetch(j):
        issue(j, j)
        pltpu.make_async_copy(column_block(before, j), block(j), bsem.at[j]).start()

    for j in range(AHEAD):
        fetch(jnp.int32(j))
    rowacc[...] = jnp.zeros_like(rowacc)
    pltpu.make_async_copy(lhs_hbm, lhs, lsem).wait()

    def step(j, carry):
        @pl.when(j + AHEAD < BLOCKS)
        def _():
            fetch(j + AHEAD)

        pltpu.make_async_copy(hid.at[j], hid.at[j], hsem.at[j]).wait()
        pltpu.make_async_copy(column_block(before, j), block(j), bsem.at[j]).wait()
        cols = pl.ds(pl.multiple_of(j * CB, CB), CB)
        col = jnp.zeros((8, CB), jnp.float32)
        for r in range(0, OWN, 384):
            g = (
                jnp.dot(lhs[r : r + 384, :], hid[j], preferred_element_type=jnp.float32)
                + whole[r : r + 384, cols]
            ) * (1.0 / ALL_TOK)
            whole[r : r + 384, cols] = g
            sq = g * g
            rowacc[r : r + 384, :] += sq[:, :128] + sq[:, 128:]
            col = col + jnp.sum(sq.reshape(48, 8, CB), axis=0)
        total = jnp.sum(col, axis=0, keepdims=True)
        cols_out[pl.ds(2 * j, 1), :] = total[:, :128]
        cols_out[pl.ds(2 * j + 1, 1), :] = total[:, 128:]
        pltpu.make_async_copy(block(j), column_block(grad, j), osem.at[j]).start()
        return carry

    lax.fori_loop(0, BLOCKS, step, 0)
    for i in range(9):
        part = rowacc[i * 128 : (i + 1) * 128, :]
        line = jnp.sum(part.T, axis=0, keepdims=True)
        for d in range(16):
            rows_out[d, i : i + 1, :] = line
    for j in range(BLOCKS):
        pltpu.make_async_copy(
            block(jnp.int32(j)), column_block(grad, jnp.int32(j)), osem.at[j]
        ).wait()


def late_product(lhs, early, pieces, pos):
    arrays, plan = numbered(pieces)
    return pl.pallas_call(
        functools.partial(late_kernel, plan, len(arrays)),
        out_shape=(
            jax.ShapeDtypeStruct((OWN, HID), jnp.float32),
            jax.ShapeDtypeStruct((16, 9, 128), jnp.float32),
            jax.ShapeDtypeStruct((18, 128), jnp.float32),
        ),
        in_specs=[SMEM] + [ANY] * (2 + len(arrays)),
        out_specs=(ANY, VMEM, VMEM),
        scratch_shapes=[
            pltpu.VMEM((OWN, LATE_TOK), jnp.bfloat16),
            pltpu.VMEM((BLOCKS, LATE_TOK, CB), jnp.bfloat16),
            pltpu.VMEM((OWN, HID), jnp.float32),
            pltpu.VMEM((OWN, 128), jnp.float32),
            pltpu.SemaphoreType.DMA,
            pltpu.SemaphoreType.DMA((BLOCKS,)),
            pltpu.SemaphoreType.DMA((BLOCKS,)),
            pltpu.SemaphoreType.DMA((BLOCKS,)),
        ],
        compiler_params=pltpu.CompilerParams(vmem_limit_bytes=LIMIT),
        cost_estimate=pl.CostEstimate(
            flops=2 * OWN * HID * LATE_TOK,
            bytes_accessed=OWN * HID * 8 + LATE_TOK * HID * 2,
            transcendentals=0,
        ),
        name="late",
    )(pos, lhs, early, *arrays)


def middle_kernel(got, row_state, cols, row_new, payload):
    row_sum = jnp.sum(got[...], axis=0)
    new = decay * row_state[...] + (1.0 - decay) * (row_sum / FFW + tiny)
    row_new[...] = new
    total = jnp.sum(jnp.sum(new, axis=0, keepdims=True), axis=1, keepdims=True)
    for d in range(16):
        payload[d, :18, :] = cols[...]
        payload[d, 18:, :] = jnp.broadcast_to(total, (6, 128))


STRIPES = 9


def update_kernel(got, row_new, col_state, grad, out, col_new, colf, gbuf, obuf, rsem, wsem):
    def read(i):
        rows = pl.ds(i * 128, 128)
        return pltpu.make_async_copy(grad.at[rows, :], gbuf.at[rows, :], rsem.at[i])

    def write(i):
        rows = pl.ds(i * 128, 128)
        return pltpu.make_async_copy(obuf.at[rows, :], out.at[rows, :], wsem.at[i])

    for i in range(AHEAD):
        read(i).start()
    sums = jnp.sum(got[...], axis=0)
    new = decay * col_state[...] + (1.0 - decay) * (sums[:18, :] / D + tiny)
    col_new[...] = new
    inv = lax.rsqrt(new)
    for k in range(18):
        colf[:, k * 128 : (k + 1) * 128] = jnp.broadcast_to(inv[k : k + 1, :], (8, 128))
    scale = sums[18:19, :] / D
    rowf = lax.rsqrt(row_new[...]) * jnp.sqrt(scale)
    for i in range(STRIPES):
        if i + AHEAD < STRIPES:
            read(i + AHEAD).start()
        column = jnp.broadcast_to(rowf[i : i + 1, :], (128, 128)).T
        read(i).wait()
        for k in range(18):
            sl = slice(k * 128, (k + 1) * 128)
            obuf[i * 128 : (i + 1) * 128, sl] = (
                gbuf[i * 128 : (i + 1) * 128, sl] * (column * colf[0:1, sl])
            ).astype(jnp.bfloat16)
        write(i).start()
    for i in range(STRIPES):
        write(i).wait()


def spread(v, axes):
    return lax.all_to_all(v, axes, 0, 0, tiled=True)


def body(pre_act, grad_out, row_state, col_state):
    pos = jnp.stack([lax.axis_index(a) for a in ("z", "yl", "x", "yh", "core")]).astype(
        jnp.int32
    )
    hidden = jax.nn.gelu(pre_act.astype(jnp.float32)).astype(jnp.bfloat16)
    grad, rows, cols = exchange(hidden, grad_out, pos)
    row_new, payload = pl.pallas_call(
        middle_kernel,
        out_shape=(
            jax.ShapeDtypeStruct((9, 128), jnp.float32),
            jax.ShapeDtypeStruct((16, 24, 128), jnp.float32),
        ),
        in_specs=[VMEM] * 3,
        out_specs=(VMEM, VMEM),
        compiler_params=pltpu.CompilerParams(vmem_limit_bytes=4 * MIB),
        name="middle",
    )(spread(rows, MP), row_state.reshape(9, 128), cols)
    update, col_new = pl.pallas_call(
        update_kernel,
        out_shape=(
            jax.ShapeDtypeStruct((OWN, HID), jnp.bfloat16),
            jax.ShapeDtypeStruct((18, 128), jnp.float32),
        ),
        in_specs=[VMEM, VMEM, VMEM, ANY],
        out_specs=(ANY, VMEM),
        scratch_shapes=[
            pltpu.VMEM((8, HID), jnp.float32),
            pltpu.VMEM((OWN, HID), jnp.float32),
            pltpu.VMEM((OWN, HID), jnp.bfloat16),
            pltpu.SemaphoreType.DMA((STRIPES,)),
            pltpu.SemaphoreType.DMA((STRIPES,)),
        ],
        compiler_params=pltpu.CompilerParams(vmem_limit_bytes=LIMIT),
        name="update",
    )(spread(payload, DP), row_new, col_state.reshape(18, 128), grad)
    return (
        update.reshape(16, WID, HID),
        row_new.reshape(16, WID),
        col_new.reshape(HID),
    )


def solution(mesh):
    fine = Mesh(mesh.devices.reshape(8, 2, 4, 2, 2), ("z", "yl", "x", "yh", "core"))
    return jax.shard_map(
        body,
        mesh=fine,
        in_specs=(P(DP, MP), P(DP, MP), P(None, DP), P(MP)),
        out_specs=(P(None, DP, MP), P(None, DP), P(MP)),
        check_vma=False,
    )
```
